1024 devices in a mesh: row: 32 (over x, z_hi, core), col: 32 (over y, z_lo).
Axes of the slice: x: 8, y: 8, z: 8 (z_hi: 2, z_lo: 4; z = z_hi * 4 + z_lo), core: 2. Of those that a mesh axis runs over, the one named last changes fastest.
Arguments:
- iterate: bfloat16 [3584, 16384], P('row', 'col'), may hold values from -0.046875 to 0.046875
- weight: float32 [3584, 16384], P('row', 'col'), may hold values from -0.625 to 0.625
Outputs:
- update: float32 [3584, 16384], P('row', 'col')
- new_weight: float32 [3584, 16384], P('row', 'col')
The draws below stay inside these ranges and needn't reach their ends.
All inputs are finite; a program needn't handle non-finite values.
Results may differ from the reference program's by a relative error of at most 0.04.
Values may be sent and summed in bfloat16 or wider, within the bound.
A program may use at most 32 MiB of HBM per device.

```python
import math
import jax
import jax.numpy as jnp

M = 3584
N = 16384


def steps_of(rng, dims, cuts, smallest, high):
    loudness = 1.0
    for position, blocks in cuts:
        steps = jax.random.uniform(jax.random.fold_in(jax.random.fold_in(rng, 6), position), (blocks,), jnp.float32, smallest / len(cuts), high / len(cuts))
        loudness = loudness * jnp.repeat(jnp.exp(steps), dims[position] // blocks).reshape((-1,) + (1,) * (len(dims) - 1 - position))
    return loudness


def scatter_about(rng, extent, width, limit, pieces=(), dtype=jnp.bfloat16):
    loudness = steps_of(rng, extent, pieces, -0.22, 0.18) if pieces else 1.0
    entries = jax.random.normal(rng, extent, jnp.float32) * width * loudness
    return jnp.minimum(jnp.maximum(entries, -limit), limit).astype(dtype)


def setup_inputs(seed: int = 0) -> dict:
    key_of = jax.random.split(jax.random.key(seed), 3)
    iterate = scatter_about(key_of[0], (M, N), N ** -0.5, 0.046875, ((0, 32), (1, 32)))
    weight = scatter_about(key_of[1], (M, N), 0.04, 0.625, ((0, 32), (1, 32)), jnp.float32)
    return dict(iterate=iterate, weight=weight)


poly_one = 3.4445
poly_three = -4.775
poly_five = 2.0315
learn_rate = 0.02
decay_rate = 0.1

def reference(iterate, weight):
    gram = jnp.dot(iterate, iterate.T, preferred_element_type=jnp.float32).astype(jnp.bfloat16)
    square = jnp.dot(gram, gram.T, preferred_element_type=jnp.float32)
    poly = (poly_three * gram.astype(jnp.float32) + poly_five * square).astype(jnp.bfloat16)
    following = poly_one * iterate.astype(jnp.float32) + jnp.dot(poly, iterate, preferred_element_type=jnp.float32)
    update = 0.2 * math.sqrt(max(M, N)) * following
    new_weight = weight * (1.0 - learn_rate * decay_rate) - learn_rate * update
    return (update, new_weight)
```

```python
import math

import jax
import jax.numpy as jnp
from jax import lax
from jax.experimental import pallas as pl
from jax.experimental.pallas import tpu as pltpu
from jax.sharding import PartitionSpec as P

M = 3584
N = 16384

poly_one = 3.4445
poly_three = -4.775
poly_five = 2.0315
learn_rate = 0.02
decay_rate = 0.1

ROWS = 112
WIDE = 128
COLS = 512
NR = 32
NC = 32
MESH = pl.DeviceIdType.MESH
F32 = jnp.float32
BF16 = jnp.bfloat16


def owner_of(slot):
    b, q = slot // 4, slot % 4
    return (2 * q + b % 2) * 4 + (q + b // 2) % 4


def slot_of(col):
    y, zl = col // 4, col % 4
    q = y // 2
    return 4 * (2 * ((zl + 4 - q) % 4) + y % 2) + q


def kernel(
    x_ref, w_ref, up_ref, nw_ref,
    xp, wp, part, prec, gram, wacc, yacc, wbf,
    rx, fx, bx, cx, ox,
    rw, fw, bw, cw, ow,
    r2, s2, r3, s3,
):
    r = lax.axis_index("row")
    c = lax.axis_index("col")
    x, zh, k = r // 4, (r // 2) % 2, r % 2

    def slot(dx, same_zh, same_core=True):
        px = (x + dx + 8) % 8
        pz = zh if same_zh else 1 - zh
        pk = k if same_core else 1 - k
        return px * 4 + pz * 2 + pk

    ahead = (slot(1, True), c)
    behind = (slot(-1, True), c)
    across = (slot(0, False), c)
    twin = (slot(0, True, False), c)

    barrier = pltpu.get_barrier_semaphore()
    for device in (ahead, behind, across, twin):
        pl.semaphore_signal(barrier, inc=1, device_id=device, device_id_type=MESH)

    def greet(i, carry):
        pl.semaphore_signal(barrier, inc=1, device_id=(r, (c + i) % NC), device_id_type=MESH)
        return carry

    lax.fori_loop(1, NC, greet, 0)
    zeros = jnp.zeros((NR, WIDE - ROWS, COLS), BF16)
    xp[:, ROWS:, :] = zeros
    wp[:, ROWS:, :] = zeros
    xp[r, :ROWS, :] = x_ref[...]
    pl.semaphore_wait(barrier, NC - 1 + 4)

    def ring(src, buf, recv, fsem, bsem, csem, osem, unit):
        def copy(source, s, send_sem, device):
            return pltpu.make_async_remote_copy(
                source, buf.at[s, pl.ds(0, ROWS)], send_sem, recv.at[s], device_id=device, device_id_type=MESH
            )

        started = []

        def send(source, s, send_sem, device):
            cp = copy(source, s, send_sem, device)
            cp.start()
            started.append(cp)

        def arrived(s):
            copy(buf.at[s, pl.ds(0, ROWS)], s, csem.at[s], twin).wait_recv()

        def forward(s, on_ahead, on_behind):
            here = buf.at[s, pl.ds(0, ROWS)]
            if on_ahead:
                send(here, s, fsem.at[s], ahead)
            if on_behind:
                send(here, s, bsem.at[s], behind)
            send(here, s, csem.at[s], twin)

        def pair(dx, same_zh):
            arrived(slot(dx, same_zh, False))
            unit(((x + dx + 8) % 8) * 2 + (zh if same_zh else 1 - zh))

        def both(d, same_zh, on_ahead, on_behind):
            lo, hi = slot(-d, same_zh), slot(d, same_zh)
            arrived(lo)
            forward(lo, on_ahead, False)
            arrived(hi)
            forward(hi, False, on_behind)

        send(src, r, osem.at[0], ahead)
        send(src, r, osem.at[1], behind)
        send(src, r, osem.at[2], across)
        send(src, r, osem.at[3], twin)
        pair(0, True)
        both(1, True, True, True)
        s = slot(0, False)
        arrived(s)
        forward(s, True, True)
        both(2, True, True, True)
        pair(-1, True)
        pair(1, True)
        both(1, False, True, True)
        pair(0, False)
        both(3, True, True, False)
        pair(-2, True)
        pair(2, True)
        both(2, False, True, True)
        pair(-1, False)
        pair(1, False)
        s = slot(-4, True)
        arrived(s)
        forward(s, False, False)
        pair(-3, True)
        pair(3, True)
        both(3, False, False, True)
        pair(-2, False)
        pair(2, False)
        s = slot(4, False)
        arrived(s)
        forward(s, False, False)
        pair(-4, True)
        pair(-3, False)
        pair(3, False)
        pair(4, False)
        return started

    mine = slot_of(c)

    def scatter(s):
        return pltpu.make_async_remote_copy(
            part.at[s], prec.at[c], s2.at[s], r2.at[c], device_id=(r, owner_of(s)), device_id_type=MESH
        )

    def gram_unit(p):
        rhs = xp[pl.ds(2 * p, 2)].reshape(2 * WIDE, COLS)
        res = lax.dot_general(x_ref[...], rhs, (((1,), (1,)), ((), ())), preferred_element_type=F32).astype(BF16)
        for h in range(2):
            s = 2 * p + h
            part[s] = res[:, h * WIDE : (h + 1) * WIDE]

            @pl.when(s != mine)
            def _():
                scatter(s).start()

    started = ring(x_ref, xp, rx, fx, bx, cx, ox, gram_unit)

    def add(i, total):
        o = (c + i) % NC
        pltpu.make_async_remote_copy(
            part.at[mine], prec.at[o], s2.at[mine], r2.at[o], device_id=(r, o), device_id_type=MESH
        ).wait_recv()
        return total + prec[o].astype(F32)

    total = lax.fori_loop(1, NC, add, part[mine].astype(F32))
    gram[mine] = total.astype(BF16)

    def spread(i):
        o = (c + i) % NC
        return pltpu.make_async_remote_copy(
            gram.at[mine], gram.at[mine], s3.at[i], r3.at[mine], device_id=(r, o), device_id_type=MESH
        )

    def spread_start(i, carry):
        spread(i).start()
        return carry

    lax.fori_loop(1, NC, spread_start, 0)

    for g in range(8):
        lhs, rhs = [], []
        for i in range(4 * g, 4 * g + 4):
            o = (c + NC - i) % NC
            s = slot_of(o)
            if i > 0:
                pltpu.make_async_remote_copy(
                    gram.at[s], gram.at[s], s3.at[i], r3.at[s], device_id=(r, o), device_id_type=MESH
                ).wait_recv()
            lhs.append(gram[s])
            rhs.append(xp[s])
        term = jnp.dot(jnp.concatenate(lhs, axis=1), jnp.concatenate(rhs, axis=0), preferred_element_type=F32)
        if g == 0:
            wacc[...] = term
        else:
            wacc[...] += term
    wbf[...] = wacc[...].astype(BF16)
    wp[r, :ROWS, :] = wbf[...]
    yacc[...] = jnp.zeros_like(yacc)

    def poly_unit(p):
        lhs = jnp.concatenate([gram[2 * p], gram[2 * p + 1]], axis=1)
        rhs = wp[pl.ds(2 * p, 2)].reshape(2 * WIDE, COLS)
        yacc[...] += jnp.dot(lhs, rhs, preferred_element_type=F32)

    started += ring(wbf, wp, rw, fw, bw, cw, ow, poly_unit)

    following = poly_one * x_ref[...].astype(F32) + poly_three * wacc[...] + poly_five * yacc[...]
    update = 0.2 * math.sqrt(max(M, N)) * following
    up_ref[...] = update
    nw_ref[...] = w_ref[...] * (1.0 - learn_rate * decay_rate) - learn_rate * update

    for cp in started:
        cp.wait_send()

    def drain(s, carry):
        @pl.when(s != mine)
        def _():
            scatter(s).wait_send()

        return carry

    lax.fori_loop(0, NR, drain, 0)

    def spread_drain(i, carry):
        spread(i).wait_send()
        return carry

    lax.fori_loop(1, NC, spread_drain, 0)


def shards(iterate, weight):
    dma = pltpu.SemaphoreType.DMA
    tile = jax.ShapeDtypeStruct((ROWS, COLS), F32)
    vmem = pl.BlockSpec(memory_space=pltpu.VMEM)
    return pl.pallas_call(
        kernel,
        out_shape=(tile, tile),
        in_specs=[vmem, vmem],
        out_specs=(vmem, vmem),
        scratch_shapes=[
            pltpu.VMEM((NR, WIDE, COLS), BF16),
            pltpu.VMEM((NR, WIDE, COLS), BF16),
            pltpu.VMEM((NR, ROWS, WIDE), BF16),
            pltpu.VMEM((NC, ROWS, WIDE), BF16),
            pltpu.VMEM((NR, ROWS, WIDE), BF16),
            pltpu.VMEM((ROWS, COLS), F32),
            pltpu.VMEM((ROWS, COLS), F32),
            pltpu.VMEM((ROWS, COLS), BF16),
        ]
        + [dma((NR,)), dma((NR,)), dma((NR,)), dma((NR,)), dma((4,))] * 2
        + [dma((NC,)), dma((NR,)), dma((NR,)), dma((NC,))],
        compiler_params=pltpu.CompilerParams(
            collective_id=0, has_side_effects=True, vmem_limit_bytes=32 * 2**20
        ),
        cost_estimate=pl.CostEstimate(flops=2 * 3 * ROWS * M * COLS, bytes_accessed=2**21, transcendentals=0),
    )(iterate, weight)


def solution(mesh):
    specs = (P("row", "col"), P("row", "col"))
    return jax.shard_map(shards, mesh=mesh, in_specs=specs, out_specs=specs, check_vma=False)
```

```python
import math

import jax
import jax.numpy as jnp
from jax import lax
from jax.experimental import pallas as pl
from jax.experimental.pallas import tpu as pltpu
from jax.sharding import PartitionSpec as P

M = 3584
N = 16384

poly_one = 3.4445
poly_three = -4.775
poly_five = 2.0315
learn_rate = 0.02
decay_rate = 0.1

ROWS = 112
WIDE = 128
COLS = 512
NR = 32
NY, NZ, NX = 8, 4, 8
CUT = 64
REST = ROWS - CUT
CHUNKS = ((0, CUT), (CUT, REST))
MESH = pl.DeviceIdType.MESH
F32 = jnp.float32
BF16 = jnp.bfloat16
AROUND = (0, 1, 7, 2, 6, 3, 5, 4)


def owner_of(slot):
    b, q = slot // 4, slot % 4
    return 2 * q + b % 2, (q + b // 2) % NZ


def slot_of(y, zl):
    q = y // 2
    return 4 * (2 * ((zl + NZ - q) % NZ) + y % 2) + q


def kernel(
    xv, out_ref,
    xp, part, pa, pb, sa, sb, qa, qb, gram, pol, bt, yacc,
    rx, fx, bx, cx, ox,
    rpa, rpb, spa, spb, rqa, rqb, sqa, sqb,
    ray, raz, say, saz, rby, rbz, sby, sbz,
    rt, st, ct, ot,
):
    r = lax.axis_index("row")
    c = lax.axis_index("col")
    x, zh, k = r // 4, (r // 2) % 2, r % 2
    y, zl = c // NZ, c % NZ

    def slot(dx, same_zh, same_core=True):
        px = (x + dx + NX) % NX
        pz = zh if same_zh else 1 - zh
        pk = k if same_core else 1 - k
        return px * 4 + pz * 2 + pk

    ahead = (slot(1, True), c)
    behind = (slot(-1, True), c)
    across = (slot(0, False), c)
    twin = (slot(0, True, False), c)

    def y_peer(i):
        return (y + i) % NY

    def z_peer(i):
        return (zl + i) % NZ

    barrier = pltpu.get_barrier_semaphore()
    peers = [across, twin]
    peers += [(slot(i, True), c) for i in range(1, NX)]
    peers += [(r, y_peer(i) * NZ + zl) for i in range(1, NY)]
    peers += [(r, y * NZ + z_peer(i)) for i in range(1, NZ)]
    for device in peers:
        pl.semaphore_signal(barrier, inc=1, device_id=device, device_id_type=MESH)
    xp[:, ROWS:, :] = jnp.zeros((NR, WIDE - ROWS, COLS), BF16)
    bt[:, ROWS:, :] = jnp.zeros((NR, WIDE - ROWS, WIDE), BF16)
    xp[r, :ROWS, :] = xv[...]
    pl.semaphore_wait(barrier, len(peers))

    def remote(src, dst, send_sem, recv_sem, device):
        return pltpu.make_async_remote_copy(src, dst, send_sem, recv_sem, device_id=device, device_id_type=MESH)

    def settle(ref, sem):
        pltpu.make_async_copy(ref, ref, sem).wait()

    started = []


    def send(source, s, h, send_sem, device):
        at, size = CHUNKS[h]
        cp = remote(source, xp.at[s, pl.ds(at, size)], send_sem, rx.at[s, h], device)
        cp.start()
        started.append(cp)

    def arrived(s, h):
        at, size = CHUNKS[h]
        settle(xp.at[s, pl.ds(at, size)], rx.at[s, h])

    def forward(s, h, on_ahead, on_behind):
        at, size = CHUNKS[h]
        here = xp.at[s, pl.ds(at, size)]
        if on_ahead:
            send(here, s, h, fx.at[s, h], ahead)
        if on_behind:
            send(here, s, h, bx.at[s, h], behind)
        send(here, s, h, cx.at[s, h], twin)

    def partial(dx, same_zh):
        other = slot(dx, same_zh, False)
        for h in range(2):
            arrived(other, h)
        p = other // 2
        rhs = xp[pl.ds(2 * p, 2)].reshape(2 * WIDE, COLS)
        res = lax.dot_general(xv[...], rhs, (((1,), (1,)), ((), ())), preferred_element_type=F32).astype(BF16)
        for h in range(2):
            s = 2 * p + h
            part[s] = res[:, h * WIDE : (h + 1) * WIDE]
            oy, oz = owner_of(s)

            @pl.when(oz != zl)
            def _():
                remote(part.at[s, pl.ds(0, CUT)], pa.at[zl, oy], spa, rpa, (r, y * NZ + oz)).start()

            @pl.when(oy != y)
            def _():
                remote(part.at[s, pl.ds(CUT, REST)], pb.at[y, oz], spb, rpb, (r, oy * NZ + zl)).start()

    def both(d, same_zh, on_ahead, on_behind):
        lo, hi = slot(-d, same_zh), slot(d, same_zh)
        for h in range(2):
            arrived(lo, h)
            forward(lo, h, on_ahead, False)
            arrived(hi, h)
            forward(hi, h, False, on_behind)

    def one(dx, same_zh, on_ahead, on_behind):
        s = slot(dx, same_zh)
        for h in range(2):
            arrived(s, h)
            forward(s, h, on_ahead, on_behind)

    for h, (at, size) in enumerate(CHUNKS):
        here = xv.at[pl.ds(at, size)]
        send(here, r, h, ox.at[2, h], across)
        send(here, r, h, ox.at[0, h], ahead)
        send(here, r, h, ox.at[1, h], behind)
        send(here, r, h, ox.at[3, h], twin)
    partial(0, True)
    both(1, True, True, True)
    one(0, False, True, True)
    both(2, True, True, True)
    partial(-1, True)
    partial(1, True)
    both(1, False, True, True)
    partial(0, False)
    both(3, True, True, False)
    partial(-2, True)
    partial(2, True)
    both(2, False, True, True)
    partial(-1, False)
    partial(1, False)
    one(-4, True, False, False)
    partial(-3, True)
    partial(3, True)
    both(3, False, False, True)
    partial(-2, False)
    partial(2, False)
    one(4, False, False, False)
    partial(-4, True)
    partial(-3, False)
    partial(3, False)
    partial(4, False)


    settle(pa.at[pl.ds(0, NZ - 1)], rpa)
    for i in AROUND:
        oy = y_peer(i)
        s = slot_of(oy, zl)
        total = part[s, :CUT].astype(F32)
        for j in range(1, NZ):
            total += pa[z_peer(j), oy].astype(F32)
        sa[i] = total.astype(BF16)
        if i:
            remote(sa.at[i], qa.at[y], sqa, rqa, (r, oy * NZ + zl)).start()
    settle(pb.at[pl.ds(0, NY - 1)], rpb)
    for j in range(NZ):
        oz = z_peer(j)
        s = slot_of(y, oz)
        total = part[s, CUT:].astype(F32)
        for i in range(1, NY):
            total += pb[y_peer(i), oz].astype(F32)
        sb[j] = total.astype(BF16)
        if j:
            remote(sb.at[j], qb.at[zl], sqb, rqb, (r, y * NZ + oz)).start()
    mine = slot_of(y, zl)
    settle(qa.at[pl.ds(0, NY - 1)], rqa)
    upper = sa[0].astype(F32)
    for i in range(1, NY):
        upper += qa[y_peer(i)].astype(F32)
    settle(qb.at[pl.ds(0, NZ - 1)], rqb)
    lower = sb[0].astype(F32)
    for j in range(1, NZ):
        lower += qb[z_peer(j)].astype(F32)
    gram[mine] = jnp.concatenate([upper, lower], axis=0).astype(BF16)


    def top(buf, s):
        return buf.at[s, pl.ds(0, CUT)]

    def low(buf, s):
        return buf.at[s, pl.ds(CUT, REST)]

    def spread(buf, n):
        def to_z(s):
            for j in range(1, NZ):
                remote(top(buf, s), top(buf, s), saz.at[n], raz.at[n, zl], (r, y * NZ + z_peer(j))).start()

        def to_y(s):
            for i in AROUND[1:]:
                remote(low(buf, s), low(buf, s), sby.at[n], rby.at[n, y], (r, y_peer(i) * NZ + zl)).start()

        for i in AROUND[1:]:
            remote(top(buf, mine), top(buf, mine), say.at[n], ray.at[n, y], (r, y_peer(i) * NZ + zl)).start()
        for j in range(1, NZ):
            remote(low(buf, mine), low(buf, mine), sbz.at[n], rbz.at[n, zl], (r, y * NZ + z_peer(j))).start()
        to_z(mine)
        to_y(mine)
        yield
        for j in range(1, NZ):
            s = slot_of(y, z_peer(j))
            settle(low(buf, s), rbz.at[n, z_peer(j)])
            to_y(s)
        for i in AROUND[1:]:
            s = slot_of(y_peer(i), zl)
            settle(top(buf, s), ray.at[n, y_peer(i)])
            to_z(s)

    def gathered(buf, n):
        for i in AROUND:
            oy = y_peer(i)
            if i == 0:
                for j in range(1, NZ):
                    settle(buf.at[pl.ds(0, NY), pl.ds(0, CUT)], raz.at[n, z_peer(j)])
            else:
                settle(buf.at[pl.ds(0, NZ), pl.ds(CUT, REST)], rby.at[n, oy])
            yield [slot_of(oy, z) for z in range(NZ)]

    def spread_done(buf, n):
        settle(buf.at[pl.ds(0, NY - 1), pl.ds(0, CUT)], say.at[n])
        settle(buf.at[pl.ds(0, NZ - 1), pl.ds(CUT, REST)], sbz.at[n])
        settle(buf.at[pl.ds(0, NY * (NZ - 1)), pl.ds(0, CUT)], saz.at[n])
        settle(buf.at[pl.ds(0, NZ * (NY - 1)), pl.ds(CUT, REST)], sby.at[n])

    def joined(buf, slots, axis):
        return jnp.concatenate([buf[s] for s in slots], axis=axis)

    steps = spread(gram, 0)
    next(steps)


    own = gram.at[mine]

    def tile(src, s, send_sem, device):
        cp = remote(src, bt.at[s, pl.ds(0, ROWS)], send_sem, rt.at[s], device)
        cp.start()
        started.append(cp)

    def tile_arrived(s):
        settle(bt.at[s, pl.ds(0, ROWS)], rt.at[s])

    bt[r, :ROWS] = gram[mine]
    tile(own, r, ot.at[0], across)
    for i in AROUND[1:]:
        tile(own, r, st.at[0, i], (slot(i, True), c))
    tile(own, r, ot.at[1], twin)
    for _ in steps:
        pass
    s = slot(0, False)
    tile_arrived(s)
    there = bt.at[s, pl.ds(0, ROWS)]
    for i in AROUND[1:]:
        tile(there, s, st.at[1, i], (slot(i, True), c))
    tile(there, s, ct.at[s], twin)
    for same in (True, False):
        for i in AROUND[1:]:
            s = slot(i, same)
            tile_arrived(s)
            tile(bt.at[s, pl.ds(0, ROWS)], s, ct.at[s], twin)
    for same in (True, False):
        for i in AROUND:
            tile_arrived(slot(i, same, False))

    square = jnp.zeros((ROWS, WIDE), F32)
    for slots in gathered(gram, 0):
        square += jnp.dot(joined(gram, slots, 1), joined(bt, slots, 0), preferred_element_type=F32)
    pol[mine] = (poly_three * gram[mine].astype(F32) + poly_five * square).astype(BF16)


    for _ in spread(pol, 1):
        pass
    yacc[...] = poly_one * xv[...].astype(F32)
    for slots in gathered(pol, 1):
        yacc[...] += jnp.dot(joined(pol, slots, 1), joined(xp, slots, 0), preferred_element_type=F32)
    out_ref[...] = yacc[...]

    for cp in started:
        cp.wait_send()
    settle(part.at[pl.ds(0, NY * (NZ - 1)), pl.ds(0, CUT)], spa)
    settle(part.at[pl.ds(0, NZ * (NY - 1)), pl.ds(CUT, REST)], spb)
    settle(sa.at[pl.ds(0, NY - 1)], sqa)
    settle(sb.at[pl.ds(0, NZ - 1)], sqb)
    spread_done(gram, 0)
    spread_done(pol, 1)


def shards(iterate, weight):
    dma = pltpu.SemaphoreType.DMA
    one = dma(())
    following = pl.pallas_call(
        kernel,
        out_shape=jax.ShapeDtypeStruct((ROWS, COLS), F32),
        in_specs=[pl.BlockSpec(memory_space=pltpu.VMEM)],
        out_specs=pl.BlockSpec(memory_space=pltpu.VMEM),
        scratch_shapes=[
            pltpu.VMEM((NR, WIDE, COLS), BF16),
            pltpu.VMEM((NR, ROWS, WIDE), BF16),
            pltpu.VMEM((NZ, NY, CUT, WIDE), BF16),
            pltpu.VMEM((NY, NZ, REST, WIDE), BF16),
            pltpu.VMEM((NY, CUT, WIDE), BF16),
            pltpu.VMEM((NZ, REST, WIDE), BF16),
            pltpu.VMEM((NY, CUT, WIDE), BF16),
            pltpu.VMEM((NZ, REST, WIDE), BF16),
            pltpu.VMEM((NR, ROWS, WIDE), BF16),
            pltpu.VMEM((NR, ROWS, WIDE), BF16),
            pltpu.VMEM((NR, WIDE, WIDE), BF16),
            pltpu.VMEM((ROWS, COLS), F32),
            dma((NR, 2)), dma((NR, 2)), dma((NR, 2)), dma((NR, 2)), dma((4, 2)),
            one, one, one, one, one, one, one, one,
            dma((2, NY)), dma((2, NZ)), dma((2,)), dma((2,)), dma((2, NY)), dma((2, NZ)), dma((2,)), dma((2,)),
            dma((NR,)), dma((2, NX)), dma((NR,)), dma((2,)),
        ],
        compiler_params=pltpu.CompilerParams(
            collective_id=0, has_side_effects=True, vmem_limit_bytes=32 * 2**20
        ),
        cost_estimate=pl.CostEstimate(flops=2 * 3 * ROWS * M * COLS, bytes_accessed=2**21, transcendentals=0),
    )(iterate)
    update = 0.2 * math.sqrt(max(M, N)) * following
    new_weight = weight * (1.0 - learn_rate * decay_rate) - learn_rate * update
    return (update, new_weight)


def solution(mesh):
    specs = (P("row", "col"), P("row", "col"))
    return jax.shard_map(shards, mesh=mesh, in_specs=specs, out_specs=specs, check_vma=False)
```

```python
import math

import jax
import jax.numpy as jnp
from jax import lax
from jax.experimental import pallas as pl
from jax.experimental.pallas import tpu as pltpu
from jax.sharding import PartitionSpec as P

M = 3584
N = 16384

poly_one = 3.4445
poly_three = -4.775
poly_five = 2.0315
learn_rate = 0.02
decay_rate = 0.1

ROWS = 112
WIDE = 128
COLS = 512
NR = 32
NY, NZ, NX = 8, 4, 8
CUT = 64
REST = ROWS - CUT
CHUNKS = ((0, CUT), (CUT, REST))
NH = len(CHUNKS)
MESH = pl.DeviceIdType.MESH
F32 = jnp.float32
BF16 = jnp.bfloat16
AROUND = (0, 1, 7, 2, 6, 3, 5, 4)


def owner_of(slot):
    b, q = slot // 4, slot % 4
    return 2 * q + b % 2, (q + b // 2) % NZ


def slot_of(y, zl):
    q = y // 2
    return 4 * (2 * ((zl + NZ - q) % NZ) + y % 2) + q


def kernel(
    xv, out_ref,
    xp, part, pa, pb, sa, sb, qa, qb, gram, pol, bt, yacc,
    rx, fx, bx, cx, ox,
    rpa, rpb, spa, spb, rqa, rqb, sqa, sqb,
    ray, raz, say, saz, rby, rbz, sby, sbz,
    rt, st, ct, ot,
):
    r = lax.axis_index("row")
    c = lax.axis_index("col")
    x, zh, k = r // 4, (r // 2) % 2, r % 2
    y, zl = c // NZ, c % NZ

    def slot(dx, same_zh, same_core=True):
        px = (x + dx + NX) % NX
        pz = zh if same_zh else 1 - zh
        pk = k if same_core else 1 - k
        return px * 4 + pz * 2 + pk

    ahead = (slot(1, True), c)
    behind = (slot(-1, True), c)
    across = (slot(0, False), c)
    twin = (slot(0, True, False), c)

    def y_peer(i):
        return (y + i) % NY

    def z_peer(i):
        return (zl + i) % NZ

    barrier = pltpu.get_barrier_semaphore()
    peers = [across, twin]
    peers += [(slot(i, True), c) for i in range(1, NX)]
    peers += [(r, y_peer(i) * NZ + zl) for i in range(1, NY)]
    peers += [(r, y * NZ + z_peer(i)) for i in range(1, NZ)]
    for device in peers:
        pl.semaphore_signal(barrier, inc=1, device_id=device, device_id_type=MESH)
    xp[:, ROWS:, :] = jnp.zeros((NR, WIDE - ROWS, COLS), BF16)
    bt[:, ROWS:, :] = jnp.zeros((NR, WIDE - ROWS, WIDE), BF16)
    xp[r, :ROWS, :] = xv[...]
    pl.semaphore_wait(barrier, len(peers))

    def remote(src, dst, send_sem, recv_sem, device):
        return pltpu.make_async_remote_copy(src, dst, send_sem, recv_sem, device_id=device, device_id_type=MESH)

    def settle(ref, sem):
        pltpu.make_async_copy(ref, ref, sem).wait()

    started = []


    def send(source, s, h, send_sem, device):
        at, size = CHUNKS[h]
        cp = remote(source, xp.at[s, pl.ds(at, size)], send_sem, rx.at[s, h], device)
        cp.start()
        started.append(cp)

    def arrived(s, h):
        at, size = CHUNKS[h]
        settle(xp.at[s, pl.ds(at, size)], rx.at[s, h])

    def forward(s, h, on_ahead, on_behind):
        at, size = CHUNKS[h]
        here = xp.at[s, pl.ds(at, size)]
        if on_ahead:
            send(here, s, h, fx.at[s, h], ahead)
        if on_behind:
            send(here, s, h, bx.at[s, h], behind)
        send(here, s, h, cx.at[s, h], twin)

    def partial(dx, same_zh):
        other = slot(dx, same_zh, False)
        for h in range(NH):
            arrived(other, h)
        p = other // 2
        rhs = xp[pl.ds(2 * p, 2)].reshape(2 * WIDE, COLS)
        res = lax.dot_general(xv[...], rhs, (((1,), (1,)), ((), ())), preferred_element_type=F32).astype(BF16)
        for h in range(2):
            s = 2 * p + h
            part[s] = res[:, h * WIDE : (h + 1) * WIDE]
            oy, oz = owner_of(s)

            @pl.when(oz != zl)
            def _():
                remote(part.at[s, pl.ds(0, CUT)], pa.at[zl, oy], spa, rpa, (r, y * NZ + oz)).start()

            @pl.when(oy != y)
            def _():
                remote(part.at[s, pl.ds(CUT, REST)], pb.at[y, oz], spb, rpb, (r, oy * NZ + zl)).start()

    def both(d, same_zh, on_ahead, on_behind):
        lo, hi = slot(-d, same_zh), slot(d, same_zh)
        for h in range(NH):
            arrived(lo, h)
            forward(lo, h, on_ahead, False)
            arrived(hi, h)
            forward(hi, h, False, on_behind)

    def one(dx, same_zh, on_ahead, on_behind):
        s = slot(dx, same_zh)
        for h in range(NH):
            arrived(s, h)
            forward(s, h, on_ahead, on_behind)

    for h, (at, size) in enumerate(CHUNKS):
        here = xv.at[pl.ds(at, size)]
        send(here, r, h, ox.at[2, h], across)
        send(here, r, h, ox.at[0, h], ahead)
        send(here, r, h, ox.at[1, h], behind)
        send(here, r, h, ox.at[3, h], twin)
    partial(0, True)
    both(1, True, True, True)
    one(0, False, True, True)
    both(2, True, True, True)
    partial(-1, True)
    partial(1, True)
    both(1, False, True, True)
    partial(0, False)
    both(3, True, True, False)
    partial(-2, True)
    partial(2, True)
    both(2, False, True, True)
    partial(-1, False)
    partial(1, False)
    one(-4, True, False, False)
    partial(-3, True)
    partial(3, True)
    both(3, False, False, True)
    partial(-2, False)
    partial(2, False)
    partial(-4, True)
    partial(-3, False)
    partial(3, False)
    one(4, False, False, False)
    partial(4, False)


    settle(pa.at[pl.ds(0, NZ - 1)], rpa)
    for i in AROUND:
        oy = y_peer(i)
        s = slot_of(oy, zl)
        total = part[s, :CUT].astype(F32)
        for j in range(1, NZ):
            total += pa[z_peer(j), oy].astype(F32)
        sa[i] = total.astype(BF16)
        if i:
            remote(sa.at[i], qa.at[y], sqa, rqa, (r, oy * NZ + zl)).start()
    settle(pb.at[pl.ds(0, NY - 1)], rpb)
    for j in range(NZ):
        oz = z_peer(j)
        s = slot_of(y, oz)
        total = part[s, CUT:].astype(F32)
        for i in range(1, NY):
            total += pb[y_peer(i), oz].astype(F32)
        sb[j] = total.astype(BF16)
        if j:
            remote(sb.at[j], qb.at[zl], sqb, rqb, (r, y * NZ + oz)).start()
    mine = slot_of(y, zl)
    settle(qa.at[pl.ds(0, NY - 1)], rqa)
    upper = sa[0].astype(F32)
    for i in range(1, NY):
        upper += qa[y_peer(i)].astype(F32)
    settle(qb.at[pl.ds(0, NZ - 1)], rqb)
    lower = sb[0].astype(F32)
    for j in range(1, NZ):
        lower += qb[z_peer(j)].astype(F32)
    gram[mine] = jnp.concatenate([upper, lower], axis=0).astype(BF16)


    def top(buf, s):
        return buf.at[s, pl.ds(0, CUT)]

    def low(buf, s):
        return buf.at[s, pl.ds(CUT, REST)]

    def to_z(buf, n, s, oy):
        for j in range(1, NZ):
            remote(top(buf, s), top(buf, s), saz.at[n], raz.at[n, zl, oy], (r, y * NZ + z_peer(j))).start()

    def to_y(buf, n, s):
        for i in AROUND[1:]:
            remote(low(buf, s), low(buf, s), sby.at[n], rby.at[n, y], (r, y_peer(i) * NZ + zl)).start()

    def spread_own(buf, n):
        for i in AROUND[1:]:
            remote(top(buf, mine), top(buf, mine), say.at[n], ray.at[n, y], (r, y_peer(i) * NZ + zl)).start()
        for j in range(1, NZ):
            remote(low(buf, mine), low(buf, mine), sbz.at[n], rbz.at[n, zl], (r, y * NZ + z_peer(j))).start()
        to_z(buf, n, mine, y)
        to_y(buf, n, mine)

    def spread_low(buf, n):
        for j in range(1, NZ):
            s = slot_of(y, z_peer(j))
            settle(low(buf, s), rbz.at[n, z_peer(j)])
            to_y(buf, n, s)

    def spread_top(buf, n):
        for i in AROUND[1:]:
            s = slot_of(y_peer(i), zl)
            settle(top(buf, s), ray.at[n, y_peer(i)])
            to_z(buf, n, s, y_peer(i))

    def gathered(buf, n):
        for i in AROUND:
            oy = y_peer(i)
            for j in range(1, NZ):
                settle(top(buf, slot_of(oy, z_peer(j))), raz.at[n, z_peer(j), oy])
            if i:
                settle(buf.at[pl.ds(0, NZ), pl.ds(CUT, REST)], rby.at[n, oy])
            yield [slot_of(oy, z) for z in range(NZ)]

    def spread_done(buf, n):
        settle(buf.at[pl.ds(0, NY - 1), pl.ds(0, CUT)], say.at[n])
        settle(buf.at[pl.ds(0, NZ - 1), pl.ds(CUT, REST)], sbz.at[n])
        settle(buf.at[pl.ds(0, NY * (NZ - 1)), pl.ds(0, CUT)], saz.at[n])
        settle(buf.at[pl.ds(0, NZ * (NY - 1)), pl.ds(CUT, REST)], sby.at[n])

    def joined(buf, slots, axis):
        return jnp.concatenate([buf[s] for s in slots], axis=axis)


    own = gram.at[mine]

    def tile(src, s, send_sem, device):
        cp = remote(src, bt.at[s, pl.ds(0, ROWS)], send_sem, rt.at[s], device)
        cp.start()
        started.append(cp)

    def tile_arrived(s):
        settle(bt.at[s, pl.ds(0, ROWS)], rt.at[s])

    bt[r, :ROWS] = gram[mine]
    tile(own, r, ot.at[0], across)
    for i in AROUND[1:]:
        tile(own, r, st.at[0, i], (slot(i, True), c))
    spread_own(gram, 0)
    tile(own, r, ot.at[1], twin)
    spread_low(gram, 0)
    s = slot(0, False)
    tile_arrived(s)
    there = bt.at[s, pl.ds(0, ROWS)]
    for i in AROUND[1:]:
        tile(there, s, st.at[1, i], (slot(i, True), c))
    tile(there, s, ct.at[s], twin)
    spread_top(gram, 0)
    square = jnp.zeros((ROWS, WIDE), F32)
    for same, half in ((True, zh), (False, 1 - zh)):
        for i in AROUND[1:]:
            s = slot(i, same)
            tile_arrived(s)
            tile(bt.at[s, pl.ds(0, ROWS)], s, ct.at[s], twin)
        for i in AROUND:
            tile_arrived(slot(i, same, False))
        for i in range(NY // 2):
            oy = half * (NY // 2) + i
            for j in range(1, NZ):
                settle(top(gram, slot_of(oy, z_peer(j))), raz.at[0, z_peer(j), oy])

            @pl.when(oy != y)
            def _():
                settle(gram.at[pl.ds(0, NZ), pl.ds(CUT, REST)], rby.at[0, oy])

            slots = [slot_of(oy, z) for z in range(NZ)]
            square += jnp.dot(joined(gram, slots, 1), joined(bt, slots, 0), preferred_element_type=F32)
    pol[mine] = (poly_three * gram[mine].astype(F32) + poly_five * square).astype(BF16)


    spread_own(pol, 1)
    spread_low(pol, 1)
    spread_top(pol, 1)
    yacc[...] = poly_one * xv[...].astype(F32)
    for cp in started:
        cp.wait_send()
    settle(part.at[pl.ds(0, NY * (NZ - 1)), pl.ds(0, CUT)], spa)
    settle(part.at[pl.ds(0, NZ * (NY - 1)), pl.ds(CUT, REST)], spb)
    settle(sa.at[pl.ds(0, NY - 1)], sqa)
    settle(sb.at[pl.ds(0, NZ - 1)], sqb)
    spread_done(gram, 0)
    for slots in gathered(pol, 1):
        yacc[...] += jnp.dot(joined(pol, slots, 1), joined(xp, slots, 0), preferred_element_type=F32)
    out_ref[...] = yacc[...]

    spread_done(pol, 1)


def shards(iterate, weight):
    dma = pltpu.SemaphoreType.DMA
    one = dma(())
    following = pl.pallas_call(
        kernel,
        out_shape=jax.ShapeDtypeStruct((ROWS, COLS), F32),
        in_specs=[pl.BlockSpec(memory_space=pltpu.VMEM)],
        out_specs=pl.BlockSpec(memory_space=pltpu.VMEM),
        scratch_shapes=[
            pltpu.VMEM((NR, WIDE, COLS), BF16),
            pltpu.VMEM((NR, ROWS, WIDE), BF16),
            pltpu.VMEM((NZ, NY, CUT, WIDE), BF16),
            pltpu.VMEM((NY, NZ, REST, WIDE), BF16),
            pltpu.VMEM((NY, CUT, WIDE), BF16),
            pltpu.VMEM((NZ, REST, WIDE), BF16),
            pltpu.VMEM((NY, CUT, WIDE), BF16),
            pltpu.VMEM((NZ, REST, WIDE), BF16),
            pltpu.VMEM((NR, ROWS, WIDE), BF16),
            pltpu.VMEM((NR, ROWS, WIDE), BF16),
            pltpu.VMEM((NR, WIDE, WIDE), BF16),
            pltpu.VMEM((ROWS, COLS), F32),
            dma((NR, NH)), dma((NR, NH)), dma((NR, NH)), dma((NR, NH)), dma((4, NH)),
            one, one, one, one, one, one, one, one,
            dma((2, NY)), dma((2, NZ, NY)), dma((2,)), dma((2,)), dma((2, NY)), dma((2, NZ)), dma((2,)), dma((2,)),
            dma((NR,)), dma((2, NX)), dma((NR,)), dma((2,)),
        ],
        compiler_params=pltpu.CompilerParams(
            collective_id=0, has_side_effects=True, vmem_limit_bytes=32 * 2**20
        ),
        cost_estimate=pl.CostEstimate(flops=2 * 3 * ROWS * M * COLS, bytes_accessed=2**21, transcendentals=0),
    )(iterate)
    update = 0.2 * math.sqrt(max(M, N)) * following
    new_weight = weight * (1.0 - learn_rate * decay_rate) - learn_rate * update
    return (update, new_weight)


def solution(mesh):
    specs = (P("row", "col"), P("row", "col"))
    return jax.shard_map(shards, mesh=mesh, in_specs=specs, out_specs=specs, check_vma=False)
```

```python
import math

import jax
import jax.numpy as jnp
from jax import lax
from jax.experimental import pallas as pl
from jax.experimental.pallas import tpu as pltpu
from jax.sharding import PartitionSpec as P

M = 3584
N = 16384

poly_one = 3.4445
poly_three = -4.775
poly_five = 2.0315
learn_rate = 0.02
decay_rate = 0.1

ROWS = 112
WIDE = 128
COLS = 512
NR = 32
NY, NZ, NX = 8, 4, 8
CUT = 64
REST = ROWS - CUT
CHUNKS = ((0, CUT), (CUT, REST))
NH = len(CHUNKS)
MESH = pl.DeviceIdType.MESH
F32 = jnp.float32
BF16 = jnp.bfloat16
AROUND = (0, 1, 7, 2, 6, 3, 5, 4)


def owner_of(slot):
    b, q = slot // 4, slot % 4
    return 2 * q + b % 2, (q + b // 2) % NZ


def slot_of(y, zl):
    q = y // 2
    return 4 * (2 * ((zl + NZ - q) % NZ) + y % 2) + q


def kernel(
    xv, out_ref,
    xp, part, pa, pb, sa, sb, qa, qb, gram, pol, bt, yacc,
    rx, fx, bx, cx, ox,
    rpa, rpb, spa, spb, rqa, rqb, sqa, sqb,
    ray, raz, say, saz, rby, rbz, sby, sbz,
    rt, st, ct, ot,
):
    r = lax.axis_index("row")
    c = lax.axis_index("col")
    x, zh, k = r // 4, (r // 2) % 2, r % 2
    y, zl = c // NZ, c % NZ

    def slot(dx, same_zh, same_core=True):
        px = (x + dx + NX) % NX
        pz = zh if same_zh else 1 - zh
        pk = k if same_core else 1 - k
        return px * 4 + pz * 2 + pk

    ahead = (slot(1, True), c)
    behind = (slot(-1, True), c)
    across = (slot(0, False), c)
    twin = (slot(0, True, False), c)

    def y_peer(i):
        return (y + i) % NY

    def z_peer(i):
        return (zl + i) % NZ

    barrier = pltpu.get_barrier_semaphore()
    peers = [across, twin]
    peers += [(slot(i, True), c) for i in range(1, NX)]
    peers += [(r, y_peer(i) * NZ + zl) for i in range(1, NY)]
    peers += [(r, y * NZ + z_peer(i)) for i in range(1, NZ)]
    for device in peers:
        pl.semaphore_signal(barrier, inc=1, device_id=device, device_id_type=MESH)
    xp[:, ROWS:, :] = jnp.zeros((NR, WIDE - ROWS, COLS), BF16)
    bt[:, ROWS:, :] = jnp.zeros((NR, WIDE - ROWS, WIDE), BF16)
    xp[r, :ROWS, :] = xv[...]
    pl.semaphore_wait(barrier, len(peers))

    def remote(src, dst, send_sem, recv_sem, device):
        return pltpu.make_async_remote_copy(src, dst, send_sem, recv_sem, device_id=device, device_id_type=MESH)

    def settle(ref, sem):
        pltpu.make_async_copy(ref, ref, sem).wait()

    started = []


    def send(source, s, h, send_sem, device):
        at, size = CHUNKS[h]
        cp = remote(source, xp.at[s, pl.ds(at, size)], send_sem, rx.at[s, h], device)
        cp.start()
        started.append(cp)

    def arrived(s, h):
        at, size = CHUNKS[h]
        settle(xp.at[s, pl.ds(at, size)], rx.at[s, h])

    def forward(s, h, on_ahead, on_behind):
        at, size = CHUNKS[h]
        here = xp.at[s, pl.ds(at, size)]
        if on_ahead:
            send(here, s, h, fx.at[s, h], ahead)
        if on_behind:
            send(here, s, h, bx.at[s, h], behind)
        send(here, s, h, cx.at[s, h], twin)

    def partial(dx, same_zh):
        other = slot(dx, same_zh, False)
        for h in range(NH):
            arrived(other, h)
        p = other // 2
        rhs = xp[pl.ds(2 * p, 2)].reshape(2 * WIDE, COLS)
        res = lax.dot_general(xv[...], rhs, (((1,), (1,)), ((), ())), preferred_element_type=F32).astype(BF16)
        for h in range(2):
            s = 2 * p + h
            part[s] = res[:, h * WIDE : (h + 1) * WIDE]
            oy, oz = owner_of(s)

            @pl.when(oz != zl)
            def _():
                remote(part.at[s, pl.ds(0, CUT)], pa.at[zl, oy], spa, rpa, (r, y * NZ + oz)).start()

            @pl.when(oy != y)
            def _():
                remote(part.at[s, pl.ds(CUT, REST)], pb.at[y, oz], spb, rpb, (r, oy * NZ + zl)).start()

    def both(d, same_zh, on_ahead, on_behind):
        lo, hi = slot(-d, same_zh), slot(d, same_zh)
        for h in range(NH):
            arrived(lo, h)
            forward(lo, h, on_ahead, False)
            arrived(hi, h)
            forward(hi, h, False, on_behind)

    def one(dx, same_zh, on_ahead, on_behind):
        s = slot(dx, same_zh)
        for h in range(NH):
            arrived(s, h)
            forward(s, h, on_ahead, on_behind)

    for h, (at, size) in enumerate(CHUNKS):
        here = xv.at[pl.ds(at, size)]
        send(here, r, h, ox.at[2, h], across)
        send(here, r, h, ox.at[0, h], ahead)
        send(here, r, h, ox.at[1, h], behind)
        send(here, r, h, ox.at[3, h], twin)
    partial(0, True)
    both(1, True, True, True)
    one(0, False, True, True)
    both(2, True, True, True)
    partial(-1, True)
    partial(1, True)
    both(1, False, True, True)
    partial(0, False)
    both(3, True, True, False)
    partial(-2, True)
    partial(2, True)
    both(2, False, True, True)
    partial(-1, False)
    partial(1, False)
    one(-4, True, False, False)
    partial(-3, True)
    partial(3, True)
    both(3, False, False, True)
    partial(-2, False)
    partial(2, False)
    partial(-4, True)
    partial(-3, False)
    partial(3, False)
    one(4, False, False, False)
    partial(4, False)


    settle(pa.at[pl.ds(0, NZ - 1)], rpa)
    for i in AROUND:
        oy = y_peer(i)
        s = slot_of(oy, zl)
        total = part[s, :CUT].astype(F32)
        for j in range(1, NZ):
            total += pa[z_peer(j), oy].astype(F32)
        sa[i] = total.astype(BF16)
        if i:
            remote(sa.at[i], qa.at[y], sqa, rqa, (r, oy * NZ + zl)).start()
    settle(pb.at[pl.ds(0, NY - 1)], rpb)
    for j in range(NZ):
        oz = z_peer(j)
        s = slot_of(y, oz)
        total = part[s, CUT:].astype(F32)
        for i in range(1, NY):
            total += pb[y_peer(i), oz].astype(F32)
        sb[j] = total.astype(BF16)
        if j:
            remote(sb.at[j], qb.at[zl], sqb, rqb, (r, y * NZ + oz)).start()
    mine = slot_of(y, zl)
    settle(qa.at[pl.ds(0, NY - 1)], rqa)
    upper = sa[0].astype(F32)
    for i in range(1, NY):
        upper += qa[y_peer(i)].astype(F32)
    settle(qb.at[pl.ds(0, NZ - 1)], rqb)
    lower = sb[0].astype(F32)
    for j in range(1, NZ):
        lower += qb[z_peer(j)].astype(F32)
    gram[mine] = jnp.concatenate([upper, lower], axis=0).astype(BF16)


    def top(buf, s):
        return buf.at[s, pl.ds(0, CUT)]

    def low(buf, s):
        return buf.at[s, pl.ds(CUT, REST)]

    def to_z(buf, n, s, oy):
        for j in range(1, NZ):
            remote(top(buf, s), top(buf, s), saz.at[n], raz.at[n, zl, oy], (r, y * NZ + z_peer(j))).start()

    def to_y(buf, n, s):
        for i in AROUND[1:]:
            remote(low(buf, s), low(buf, s), sby.at[n], rby.at[n, y], (r, y_peer(i) * NZ + zl)).start()

    def spread_own(buf, n):
        for i in AROUND[1:]:
            remote(top(buf, mine), top(buf, mine), say.at[n], ray.at[n, y], (r, y_peer(i) * NZ + zl)).start()
        for j in range(1, NZ):
            remote(low(buf, mine), low(buf, mine), sbz.at[n], rbz.at[n, zl], (r, y * NZ + z_peer(j))).start()
        to_z(buf, n, mine, y)
        to_y(buf, n, mine)

    def spread_low(buf, n):
        for j in range(1, NZ):
            s = slot_of(y, z_peer(j))
            settle(low(buf, s), rbz.at[n, z_peer(j)])
            to_y(buf, n, s)

    def spread_top(buf, n):
        for i in AROUND[1:]:
            s = slot_of(y_peer(i), zl)
            settle(top(buf, s), ray.at[n, y_peer(i)])
            to_z(buf, n, s, y_peer(i))

    def gathered(buf, n):
        for i in AROUND:
            oy = y_peer(i)
            for j in range(1, NZ):
                settle(top(buf, slot_of(oy, z_peer(j))), raz.at[n, z_peer(j), oy])
            if i:
                settle(buf.at[pl.ds(0, NZ), pl.ds(CUT, REST)], rby.at[n, oy])
            yield [slot_of(oy, z) for z in range(NZ)]

    def spread_done(buf, n):
        settle(buf.at[pl.ds(0, NY - 1), pl.ds(0, CUT)], say.at[n])
        settle(buf.at[pl.ds(0, NZ - 1), pl.ds(CUT, REST)], sbz.at[n])
        settle(buf.at[pl.ds(0, NY * (NZ - 1)), pl.ds(0, CUT)], saz.at[n])
        settle(buf.at[pl.ds(0, NZ * (NY - 1)), pl.ds(CUT, REST)], sby.at[n])

    def joined(buf, slots, axis):
        return jnp.concatenate([buf[s] for s in slots], axis=axis)


    own = gram.at[mine]

    def tile(src, s, send_sem, device):
        cp = remote(src, bt.at[s, pl.ds(0, ROWS)], send_sem, rt.at[s], device)
        cp.start()
        started.append(cp)

    def tile_arrived(s):
        settle(bt.at[s, pl.ds(0, ROWS)], rt.at[s])

    bt[r, :ROWS] = gram[mine]
    tile(own, r, ot.at[0], across)
    for i in AROUND[1:]:
        tile(own, r, st.at[0, i], (slot(i, True), c))
    spread_own(gram, 0)
    tile(own, r, ot.at[1], twin)
    spread_low(gram, 0)
    s = slot(0, False)
    tile_arrived(s)
    there = bt.at[s, pl.ds(0, ROWS)]
    for i in AROUND[1:]:
        tile(there, s, st.at[1, i], (slot(i, True), c))
    tile(there, s, ct.at[s], twin)
    spread_top(gram, 0)
    square = jnp.zeros((ROWS, WIDE), F32)
    for same, half in ((True, zh), (False, 1 - zh)):
        for i in AROUND[1:]:
            s = slot(i, same)
            tile_arrived(s)
            tile(bt.at[s, pl.ds(0, ROWS)], s, ct.at[s], twin)
    for same, half in ((True, zh), (False, 1 - zh)):
        for i in AROUND:
            tile_arrived(slot(i, same, False))
        for i in range(NY // 2):
            oy = half * (NY // 2) + i
            for j in range(1, NZ):
                settle(top(gram, slot_of(oy, z_peer(j))), raz.at[0, z_peer(j), oy])

            @pl.when(oy != y)
            def _():
                settle(gram.at[pl.ds(0, NZ), pl.ds(CUT, REST)], rby.at[0, oy])

            slots = [slot_of(oy, z) for z in range(NZ)]
            square += jnp.dot(joined(gram, slots, 1), joined(bt, slots, 0), preferred_element_type=F32)
    pol[mine] = (poly_three * gram[mine].astype(F32) + poly_five * square).astype(BF16)


    spread_own(pol, 1)
    spread_low(pol, 1)
    spread_top(pol, 1)
    yacc[...] = poly_one * xv[...].astype(F32)
    for cp in started:
        cp.wait_send()
    settle(part.at[pl.ds(0, NY * (NZ - 1)), pl.ds(0, CUT)], spa)
    settle(part.at[pl.ds(0, NZ * (NY - 1)), pl.ds(CUT, REST)], spb)
    settle(sa.at[pl.ds(0, NY - 1)], sqa)
    settle(sb.at[pl.ds(0, NZ - 1)], sqb)
    spread_done(gram, 0)
    for slots in gathered(pol, 1):
        yacc[...] += jnp.dot(joined(pol, slots, 1), joined(xp, slots, 0), preferred_element_type=F32)
    out_ref[...] = yacc[...]

    spread_done(pol, 1)


def shards(iterate, weight):
    dma = pltpu.SemaphoreType.DMA
    one = dma(())
    following = pl.pallas_call(
        kernel,
        out_shape=jax.ShapeDtypeStruct((ROWS, COLS), F32),
        in_specs=[pl.BlockSpec(memory_space=pltpu.VMEM)],
        out_specs=pl.BlockSpec(memory_space=pltpu.VMEM),
        scratch_shapes=[
            pltpu.VMEM((NR, WIDE, COLS), BF16),
            pltpu.VMEM((NR, ROWS, WIDE), BF16),
            pltpu.VMEM((NZ, NY, CUT, WIDE), BF16),
            pltpu.VMEM((NY, NZ, REST, WIDE), BF16),
            pltpu.VMEM((NY, CUT, WIDE), BF16),
            pltpu.VMEM((NZ, REST, WIDE), BF16),
            pltpu.VMEM((NY, CUT, WIDE), BF16),
            pltpu.VMEM((NZ, REST, WIDE), BF16),
            pltpu.VMEM((NR, ROWS, WIDE), BF16),
            pltpu.VMEM((NR, ROWS, WIDE), BF16),
            pltpu.VMEM((NR, WIDE, WIDE), BF16),
            pltpu.VMEM((ROWS, COLS), F32),
            dma((NR, NH)), dma((NR, NH)), dma((NR, NH)), dma((NR, NH)), dma((4, NH)),
            one, one, one, one, one, one, one, one,
            dma((2, NY)), dma((2, NZ, NY)), dma((2,)), dma((2,)), dma((2, NY)), dma((2, NZ)), dma((2,)), dma((2,)),
            dma((NR,)), dma((2, NX)), dma((NR,)), dma((2,)),
        ],
        compiler_params=pltpu.CompilerParams(
            collective_id=0, has_side_effects=True, vmem_limit_bytes=32 * 2**20
        ),
        cost_estimate=pl.CostEstimate(flops=2 * 3 * ROWS * M * COLS, bytes_accessed=2**21, transcendentals=0),
    )(iterate)
    update = 0.2 * math.sqrt(max(M, N)) * following
    new_weight = weight * (1.0 - learn_rate * decay_rate) - learn_rate * update
    return (update, new_weight)


def solution(mesh):
    specs = (P("row", "col"), P("row", "col"))
    return jax.shard_map(shards, mesh=mesh, in_specs=specs, out_specs=specs, check_vma=False)
```

```python
import math

import jax
import jax.numpy as jnp
from jax import lax
from jax.experimental import pallas as pl
from jax.experimental.pallas import tpu as pltpu
from jax.sharding import PartitionSpec as P

M = 3584
N = 16384

poly_one = 3.4445
poly_three = -4.775
poly_five = 2.0315
learn_rate = 0.02
decay_rate = 0.1

ROWS = 112
WIDE = 128
COLS = 512
NR = 32
NY, NZ, NX = 8, 4, 8
CUT = 64
REST = ROWS - CUT
CHUNKS = ((0, CUT), (CUT, REST))
NH = len(CHUNKS)
MESH = pl.DeviceIdType.MESH
F32 = jnp.float32
BF16 = jnp.bfloat16
AROUND = (0, 1, 7, 2, 6, 3, 5, 4)
FAR_FIRST = AROUND[:0:-1]


def owner_of(slot):
    b, q = slot // 4, slot % 4
    return 2 * q + b % 2, (q + b // 2) % NZ


def slot_of(y, zl):
    q = y // 2
    return 4 * (2 * ((zl + NZ - q) % NZ) + y % 2) + q


def kernel(
    xv, out_ref,
    xp, part, pa, pb, sa, sb, qa, qb, gram, pol, bt, yacc,
    rx, fx, bx, cx, ox,
    rpa, rpb, spa, spb, rqa, rqb, sqa, sqb,
    ray, raz, say, saz, rby, rbz, sby, sbz,
    rt, st, ct, ot,
):
    r = lax.axis_index("row")
    c = lax.axis_index("col")
    x, zh, k = r // 4, (r // 2) % 2, r % 2
    y, zl = c // NZ, c % NZ

    def slot(dx, same_zh, same_core=True):
        px = (x + dx + NX) % NX
        pz = zh if same_zh else 1 - zh
        pk = k if same_core else 1 - k
        return px * 4 + pz * 2 + pk

    ahead = (slot(1, True), c)
    behind = (slot(-1, True), c)
    across = (slot(0, False), c)
    twin = (slot(0, True, False), c)

    def y_peer(i):
        return (y + i) % NY

    def z_peer(i):
        return (zl + i) % NZ

    barrier = pltpu.get_barrier_semaphore()
    peers = [across, twin]
    peers += [(slot(i, True), c) for i in range(1, NX)]
    peers += [(r, y_peer(i) * NZ + zl) for i in range(1, NY)]
    peers += [(r, y * NZ + z_peer(i)) for i in range(1, NZ)]
    for device in peers:
        pl.semaphore_signal(barrier, inc=1, device_id=device, device_id_type=MESH)
    xp[:, ROWS:, :] = jnp.zeros((NR, WIDE - ROWS, COLS), BF16)
    bt[:, ROWS:, :] = jnp.zeros((NR, WIDE - ROWS, WIDE), BF16)
    xp[r, :ROWS, :] = xv[...]
    pl.semaphore_wait(barrier, len(peers))

    def remote(src, dst, send_sem, recv_sem, device):
        return pltpu.make_async_remote_copy(src, dst, send_sem, recv_sem, device_id=device, device_id_type=MESH)

    def settle(ref, sem):
        pltpu.make_async_copy(ref, ref, sem).wait()

    started = []


    def send(source, s, h, send_sem, device):
        at, size = CHUNKS[h]
        cp = remote(source, xp.at[s, pl.ds(at, size)], send_sem, rx.at[s, h], device)
        cp.start()
        started.append(cp)

    def arrived(s, h):
        at, size = CHUNKS[h]
        settle(xp.at[s, pl.ds(at, size)], rx.at[s, h])

    def forward(s, h, on_ahead, on_behind):
        at, size = CHUNKS[h]
        here = xp.at[s, pl.ds(at, size)]
        if on_ahead:
            send(here, s, h, fx.at[s, h], ahead)
        if on_behind:
            send(here, s, h, bx.at[s, h], behind)
        send(here, s, h, cx.at[s, h], twin)

    def partial(dx, same_zh):
        other = slot(dx, same_zh, False)
        for h in range(NH):
            arrived(other, h)
        p = other // 2
        rhs = xp[pl.ds(2 * p, 2)].reshape(2 * WIDE, COLS)
        res = lax.dot_general(xv[...], rhs, (((1,), (1,)), ((), ())), preferred_element_type=F32).astype(BF16)
        for h in range(2):
            s = 2 * p + h
            part[s] = res[:, h * WIDE : (h + 1) * WIDE]
            oy, oz = owner_of(s)

            @pl.when(oz != zl)
            def _():
                remote(part.at[s, pl.ds(0, CUT)], pa.at[zl, oy], spa, rpa, (r, y * NZ + oz)).start()

            @pl.when(oy != y)
            def _():
                remote(part.at[s, pl.ds(CUT, REST)], pb.at[y, oz], spb, rpb, (r, oy * NZ + zl)).start()

    def both(d, same_zh, on_ahead, on_behind):
        lo, hi = slot(-d, same_zh), slot(d, same_zh)
        for h in range(NH):
            arrived(lo, h)
            forward(lo, h, on_ahead, False)
            arrived(hi, h)
            forward(hi, h, False, on_behind)

    def one(dx, same_zh, on_ahead, on_behind):
        s = slot(dx, same_zh)
        for h in range(NH):
            arrived(s, h)
            forward(s, h, on_ahead, on_behind)

    for h, (at, size) in enumerate(CHUNKS):
        here = xv.at[pl.ds(at, size)]
        send(here, r, h, ox.at[2, h], across)
        send(here, r, h, ox.at[0, h], ahead)
        send(here, r, h, ox.at[1, h], behind)
        send(here, r, h, ox.at[3, h], twin)
    partial(0, True)
    both(1, True, True, True)
    one(0, False, True, True)
    both(2, True, True, True)
    partial(-1, True)
    partial(1, True)
    both(1, False, True, True)
    partial(0, False)
    both(3, True, True, False)
    partial(-2, True)
    partial(2, True)
    both(2, False, True, True)
    partial(-1, False)
    partial(1, False)
    one(-4, True, False, False)
    partial(-3, True)
    partial(3, True)
    both(3, False, False, True)
    partial(-2, False)
    partial(2, False)
    partial(-4, True)
    partial(-3, False)
    partial(3, False)
    one(4, False, False, False)
    partial(4, False)


    settle(pa.at[pl.ds(0, NZ - 1)], rpa)
    for i in (*FAR_FIRST, 0):
        oy = y_peer(i)
        s = slot_of(oy, zl)
        total = part[s, :CUT].astype(F32)
        for j in range(1, NZ):
            total += pa[z_peer(j), oy].astype(F32)
        sa[i] = total.astype(BF16)
        if i:
            remote(sa.at[i], qa.at[y], sqa, rqa, (r, oy * NZ + zl)).start()
    settle(pb.at[pl.ds(0, NY - 1)], rpb)
    for j in range(NZ):
        oz = z_peer(j)
        s = slot_of(y, oz)
        total = part[s, CUT:].astype(F32)
        for i in range(1, NY):
            total += pb[y_peer(i), oz].astype(F32)
        sb[j] = total.astype(BF16)
        if j:
            remote(sb.at[j], qb.at[zl], sqb, rqb, (r, y * NZ + oz)).start()
    mine = slot_of(y, zl)
    settle(qa.at[pl.ds(0, NY - 1)], rqa)
    upper = sa[0].astype(F32)
    for i in range(1, NY):
        upper += qa[y_peer(i)].astype(F32)
    settle(qb.at[pl.ds(0, NZ - 1)], rqb)
    lower = sb[0].astype(F32)
    for j in range(1, NZ):
        lower += qb[z_peer(j)].astype(F32)
    gram[mine] = jnp.concatenate([upper, lower], axis=0).astype(BF16)


    def top(buf, s):
        return buf.at[s, pl.ds(0, CUT)]

    def low(buf, s):
        return buf.at[s, pl.ds(CUT, REST)]

    def to_z(buf, n, s, oy):
        for j in range(1, NZ):
            remote(top(buf, s), top(buf, s), saz.at[n], raz.at[n, zl, oy], (r, y * NZ + z_peer(j))).start()

    def to_y(buf, n, s):
        for i in FAR_FIRST:
            remote(low(buf, s), low(buf, s), sby.at[n], rby.at[n, y], (r, y_peer(i) * NZ + zl)).start()

    def spread_own(buf, n):
        for i in FAR_FIRST:
            remote(top(buf, mine), top(buf, mine), say.at[n], ray.at[n, y], (r, y_peer(i) * NZ + zl)).start()
        for j in range(1, NZ):
            remote(low(buf, mine), low(buf, mine), sbz.at[n], rbz.at[n, zl], (r, y * NZ + z_peer(j))).start()
        to_z(buf, n, mine, y)
        to_y(buf, n, mine)

    def spread_low(buf, n):
        for j in range(1, NZ):
            s = slot_of(y, z_peer(j))
            settle(low(buf, s), rbz.at[n, z_peer(j)])
            to_y(buf, n, s)

    def spread_top(buf, n):
        for i in AROUND[1:]:
            s = slot_of(y_peer(i), zl)
            settle(top(buf, s), ray.at[n, y_peer(i)])
            to_z(buf, n, s, y_peer(i))

    def gathered(buf, n):
        for i in AROUND:
            oy = y_peer(i)
            for j in range(1, NZ):
                settle(top(buf, slot_of(oy, z_peer(j))), raz.at[n, z_peer(j), oy])
            if i:
                settle(buf.at[pl.ds(0, NZ), pl.ds(CUT, REST)], rby.at[n, oy])
            yield [slot_of(oy, z) for z in range(NZ)]

    def spread_done(buf, n):
        settle(buf.at[pl.ds(0, NY - 1), pl.ds(0, CUT)], say.at[n])
        settle(buf.at[pl.ds(0, NZ - 1), pl.ds(CUT, REST)], sbz.at[n])
        settle(buf.at[pl.ds(0, NY * (NZ - 1)), pl.ds(0, CUT)], saz.at[n])
        settle(buf.at[pl.ds(0, NZ * (NY - 1)), pl.ds(CUT, REST)], sby.at[n])

    def joined(buf, slots, axis):
        return jnp.concatenate([buf[s] for s in slots], axis=axis)


    own = gram.at[mine]

    def tile(src, s, send_sem, device):
        cp = remote(src, bt.at[s, pl.ds(0, ROWS)], send_sem, rt.at[s], device)
        cp.start()
        started.append(cp)

    def tile_arrived(s):
        settle(bt.at[s, pl.ds(0, ROWS)], rt.at[s])

    bt[r, :ROWS] = gram[mine]
    tile(own, r, ot.at[0], across)
    for i in FAR_FIRST:
        tile(own, r, st.at[0, i], (slot(i, True), c))
    spread_own(gram, 0)
    tile(own, r, ot.at[1], twin)
    spread_low(gram, 0)
    s = slot(0, False)
    tile_arrived(s)
    there = bt.at[s, pl.ds(0, ROWS)]
    for i in FAR_FIRST:
        tile(there, s, st.at[1, i], (slot(i, True), c))
    tile(there, s, ct.at[s], twin)
    spread_top(gram, 0)
    square = jnp.zeros((ROWS, WIDE), F32)
    for same, half in ((True, zh), (False, 1 - zh)):
        for i in AROUND[1:]:
            s = slot(i, same)
            tile_arrived(s)
            tile(bt.at[s, pl.ds(0, ROWS)], s, ct.at[s], twin)
    for same, half in ((True, zh), (False, 1 - zh)):
        for i in AROUND:
            tile_arrived(slot(i, same, False))
        for i in range(NY // 2):
            oy = half * (NY // 2) + i
            for j in range(1, NZ):
                settle(top(gram, slot_of(oy, z_peer(j))), raz.at[0, z_peer(j), oy])

            @pl.when(oy != y)
            def _():
                settle(gram.at[pl.ds(0, NZ), pl.ds(CUT, REST)], rby.at[0, oy])

            slots = [slot_of(oy, z) for z in range(NZ)]
            square += jnp.dot(joined(gram, slots, 1), joined(bt, slots, 0), preferred_element_type=F32)
    pol[mine] = (poly_three * gram[mine].astype(F32) + poly_five * square).astype(BF16)


    spread_own(pol, 1)
    spread_low(pol, 1)
    spread_top(pol, 1)
    yacc[...] = poly_one * xv[...].astype(F32)
    for cp in started:
        cp.wait_send()
    settle(part.at[pl.ds(0, NY * (NZ - 1)), pl.ds(0, CUT)], spa)
    settle(part.at[pl.ds(0, NZ * (NY - 1)), pl.ds(CUT, REST)], spb)
    settle(sa.at[pl.ds(0, NY - 1)], sqa)
    settle(sb.at[pl.ds(0, NZ - 1)], sqb)
    spread_done(gram, 0)
    for slots in gathered(pol, 1):
        yacc[...] += jnp.dot(joined(pol, slots, 1), joined(xp, slots, 0), preferred_element_type=F32)
    out_ref[...] = yacc[...]

    spread_done(pol, 1)


def shards(iterate, weight):
    dma = pltpu.SemaphoreType.DMA
    one = dma(())
    following = pl.pallas_call(
        kernel,
        out_shape=jax.ShapeDtypeStruct((ROWS, COLS), F32),
        in_specs=[pl.BlockSpec(memory_space=pltpu.VMEM)],
        out_specs=pl.BlockSpec(memory_space=pltpu.VMEM),
        scratch_shapes=[
            pltpu.VMEM((NR, WIDE, COLS), BF16),
            pltpu.VMEM((NR, ROWS, WIDE), BF16),
            pltpu.VMEM((NZ, NY, CUT, WIDE), BF16),
            pltpu.VMEM((NY, NZ, REST, WIDE), BF16),
            pltpu.VMEM((NY, CUT, WIDE), BF16),
            pltpu.VMEM((NZ, REST, WIDE), BF16),
            pltpu.VMEM((NY, CUT, WIDE), BF16),
            pltpu.VMEM((NZ, REST, WIDE), BF16),
            pltpu.VMEM((NR, ROWS, WIDE), BF16),
            pltpu.VMEM((NR, ROWS, WIDE), BF16),
            pltpu.VMEM((NR, WIDE, WIDE), BF16),
            pltpu.VMEM((ROWS, COLS), F32),
            dma((NR, NH)), dma((NR, NH)), dma((NR, NH)), dma((NR, NH)), dma((4, NH)),
            one, one, one, one, one, one, one, one,
            dma((2, NY)), dma((2, NZ, NY)), dma((2,)), dma((2,)), dma((2, NY)), dma((2, NZ)), dma((2,)), dma((2,)),
            dma((NR,)), dma((2, NX)), dma((NR,)), dma((2,)),
        ],
        compiler_params=pltpu.CompilerParams(
            collective_id=0, has_side_effects=True, vmem_limit_bytes=32 * 2**20
        ),
        cost_estimate=pl.CostEstimate(flops=2 * 3 * ROWS * M * COLS, bytes_accessed=2**21, transcendentals=0),
    )(iterate)
    update = 0.2 * math.sqrt(max(M, N)) * following
    new_weight = weight * (1.0 - learn_rate * decay_rate) - learn_rate * update
    return (update, new_weight)


def solution(mesh):
    specs = (P("row", "col"), P("row", "col"))
    return jax.shard_map(shards, mesh=mesh, in_specs=specs, out_specs=specs, check_vma=False)
```
